512 devices in a mesh: row: 16 (over z_lo, x), col: 32 (over y, z_hi, core).
Axes of the slice: x: 4, y: 4, z: 16 (z_hi: 4, z_lo: 4; z = z_hi * 4 + z_lo), core: 2. Of those that a mesh axis runs over, the one named last changes fastest.
Arguments:
- features: bfloat16 [131072, 128], P(('col', 'row')), may hold values from -6 to 6
- weight: bfloat16 [128, 128], replicated, may hold values from -0.5 to 0.5
- tile_values: bfloat16 [16, 32, 16, 128, 128], P('row', 'col'), may hold values from -0.1875 to 0.1875
- tile_rows: int32 [16, 32, 16], P('row', 'col'), may hold values from 0 to 63, as said below
- tile_cols: int32 [16, 32, 16], P('row', 'col'), may hold values from 0 to 31
- tile_count: int32 [16, 32], P('row', 'col'), may hold values from 4 to 16, as said below
- node_order: int32 [131072], P(('row', 'col')), may hold values from 0 to 131071, as said below
Outputs:
- activated: bfloat16 [131072, 128], P(('row', 'col'))
The draws below stay inside these ranges and needn't reach their ends.
Inputs may be any that keep to these rules, and one draw needn't show every extreme that they name: `tile_count`: every grid cell uses at least 4 slots; in every grid row some cell uses all 16. `tile_rows`: within one grid cell, no two slots name tile rows of the same aligned block of 2 tile rows. `node_order`: A permutation that maps each aligned block of 256 nodes onto itself.
All inputs are finite; a program needn't handle non-finite values.
Results may differ from the reference program's by a relative error of at most 0.0049.
Values may be sent and summed in bfloat16 or wider, within the bound.
A program may use at most 64 MiB of HBM per device.

```python
import jax
import jax.numpy as jnp
from jax import lax

F = 128
TILE = 128
TILES_DEV = 2
MAXT = 16
NODES = 131072
N_ROW = 16
N_COL = 32


def draw_tile_rows(key, part):
    key = jax.random.fold_in(key, 5)
    owner_key, within_key = jax.random.split(key)
    cell_keys = jax.random.split(owner_key, N_ROW * N_COL)
    owners = jax.vmap(lambda k: jax.random.permutation(k, N_COL)[:MAXT])(cell_keys)
    owners = owners.reshape(N_ROW, N_COL, MAXT)
    within = jax.random.randint(within_key, (N_ROW, N_COL, MAXT), 0, TILES_DEV)
    return (owners * TILES_DEV + within).astype(jnp.int32)


def draw_tile_count(key, part):
    key = jax.random.fold_in(key, 11)
    counts = jax.random.randint(key, (N_ROW, N_COL), MAXT // 4, MAXT + 1)
    row_ids = jnp.arange(N_ROW)[:, None]
    col_ids = jnp.arange(N_COL)[None, :]
    full = col_ids == row_ids % N_COL
    return jnp.where(full, MAXT, counts).astype(jnp.int32)


def draw_node_order(key, part):
    key = jax.random.fold_in(key, 23)
    block_rows = TILES_DEV * TILE
    block_total = NODES // block_rows
    keys = jax.random.split(key, block_total)
    orders = jax.vmap(lambda k: jax.random.permutation(k, block_rows))(keys)
    starts = jnp.arange(block_total)[:, None] * block_rows
    return (orders + starts).reshape(-1).astype(jnp.int32)


def touch_ends(array, rng, least, top_value):
    longest = array.shape.index(max(array.shape))
    spots = []
    for shift in (0, 1):
        where = [jax.random.randint(jax.random.fold_in(rng, axis), (), 0, length) for axis, length in enumerate(array.shape)]
        where[longest] = (where[longest] + shift) % array.shape[longest]
        spots.append(tuple(where))
    return array.at[spots[0]].set(least).at[spots[1]].set(top_value)


def block_scale(key, shape, pieces, smallest, top_value):
    def one(axis_at, parts):
        heights = jax.random.uniform(jax.random.fold_in(jax.random.fold_in(key, 6), axis_at), (parts,), jnp.float32, smallest / len(pieces), top_value / len(pieces))
        return jnp.repeat(jnp.exp(heights), shape[axis_at] // parts).reshape((-1,) + (1,) * (len(shape) - axis_at - 1))

    factor_of = one(*pieces[0])
    for cut in pieces[1:]:
        factor_of = factor_of * one(*cut)
    return factor_of


def bell_draw(own_key, extent, spread, limit, shards=(), kind=jnp.bfloat16):
    loudness = block_scale(own_key, extent, shards, -0.22, 0.18) if shards else 1.0
    values = jax.random.normal(own_key, extent, jnp.float32) * spread * loudness
    return jnp.minimum(jnp.maximum(values, -limit), limit).astype(kind)


def setup_inputs(seed: int = 0) -> dict:
    seeds = jax.random.split(jax.random.key(seed), 8)
    return {
        "features": bell_draw(seeds[0], (NODES, F), 1.0, 6.0, ((0, 512),)),
        "weight": bell_draw(seeds[1], (F, F), F ** -0.5, 0.5),
        "tile_values": bell_draw(seeds[2], (N_ROW, N_COL, MAXT, TILE, TILE), (TILE * MAXT // TILES_DEV) ** -0.5, 0.1875, ((0, 16), (1, 32))),
        "tile_rows": draw_tile_rows(jax.random.fold_in(seeds[7], 71), 0),
        "tile_cols": touch_ends(jax.random.randint(seeds[4], (N_ROW, N_COL, MAXT), 0, TILES_DEV * N_ROW), jax.random.fold_in(seeds[4], 1), 0, (TILES_DEV * N_ROW) - 1).astype(jnp.int32),
        "tile_count": draw_tile_count(jax.random.fold_in(seeds[7], 71), 0),
        "node_order": draw_node_order(jax.random.fold_in(seeds[7], 71), 0),
    }


def reference(features, weight, tile_values, tile_rows, tile_cols, tile_count, node_order):
    rows_block = TILES_DEV * N_COL
    cols_block = TILES_DEV * N_ROW
    xtiles = features.reshape(NODES // TILE, TILE, F)

    def row_block_sum(row_block):
        tile_vals = tile_values[row_block].astype(jnp.float32)
        offsets = (jnp.arange(N_COL).astype(jnp.int32) * cols_block).astype(jnp.int32)
        column_ids = (tile_cols[row_block] + offsets[:, None]).astype(jnp.int32)
        inputs = xtiles[column_ids].astype(jnp.float32)
        products = jnp.einsum("cktu,ckuf->cktf", tile_vals, inputs)
        active = jnp.arange(MAXT).astype(jnp.int32)[None, :] < tile_count[row_block][:, None]
        products = jnp.where(active[:, :, None, None], products, jnp.zeros((), jnp.float32))
        summed = jax.ops.segment_sum(products.reshape(N_COL * MAXT, TILE, F), tile_rows[row_block].reshape(-1), num_segments=rows_block)
        return summed.reshape(rows_block * TILE, F)

    aggregated = lax.map(row_block_sum, jnp.arange(N_ROW).astype(jnp.int32)).reshape(NODES, F)
    aggregated_low = aggregated.astype(jnp.bfloat16)
    mixed = jnp.maximum(jnp.dot(aggregated_low, weight, preferred_element_type=jnp.float32), 0.0).astype(jnp.bfloat16)
    return jnp.zeros_like(mixed).at[node_order].set(mixed)
```

```python
import functools

import jax
import jax.numpy as jnp
from jax import lax
from jax.experimental import pallas as pl
from jax.experimental.pallas import tpu as pltpu
from jax.sharding import PartitionSpec as P

MESH = pl.DeviceIdType.MESH
TILE = 128
SLOTS = 16
LINE = 4
FAR_FIRST = (2, 1, 3, 0)
RING = tuple((dy, dc) for dy in FAR_FIRST for dc in (1, 0))
OTHERS = RING[:-1]


def kernel(
    features,
    weight,
    tile_values,
    tile_rows,
    tile_cols,
    tile_count,
    node_order,
    out,
    gathered,
    tiles,
    products,
    flags_out,
    flags_in,
    ring_out,
    ring_in,
    sums_out,
    sums_in,
    tiles_sem,
    gather_send,
    gather_recv,
    flags_send,
    flags_recv,
    ring_send,
    ring_recv,
    sums_send,
    sums_recv,
):
    row, col = lax.axis_index("row"), lax.axis_index("col")
    z, x = row // LINE, row % LINE
    y, h, core = col // 8, (col // 2) % LINE, col % 2

    def in_row(z_at, x_at):
        return (z_at * LINE + x_at, col)

    def in_col(dy, dh, dc):
        return (row, ((y + dy) % LINE) * 8 + ((h + dh) % LINE) * 2 + (core + dc) % 2)

    def send(src, dst, send_sem, recv_sem, device):
        copy = pltpu.make_async_remote_copy(
            src_ref=src, dst_ref=dst, send_sem=send_sem, recv_sem=recv_sem, device_id=device, device_id_type=MESH
        )
        copy.start()
        return copy

    pending = []

    load_tiles = pltpu.make_async_copy(tile_values.at[0, 0], tiles, tiles_sem.at[0])
    load_tiles.start()
    load_mine = pltpu.make_async_copy(features, gathered.at[pl.ds(2 * row, 2)], tiles_sem.at[1])
    load_mine.start()

    barrier = pltpu.get_barrier_semaphore()
    partners = (
        [in_row((z + d) % LINE, x) for d in (1, 2, 3)]
        + [in_row(z, (x + d) % LINE) for d in (1, 2, 3)]
        + [in_col(dy, 0, dc) for dy, dc in OTHERS]
        + [in_col(0, dh, 0) for dh in (1, 2, 3)]
    )
    for device in partners:
        pl.semaphore_signal(barrier, inc=1, device_id=device, device_id_type=MESH)
    pl.semaphore_wait(barrier, len(partners))

    def block(z_at, x_at):
        return gathered.at[pl.ds(2 * (z_at * LINE + x_at), 2)]

    sends = 0
    for d in (1, 3, 2):
        pending.append(
            send(features, block(z, x), gather_send.at[sends], gather_recv.at[row], in_row((z + d) % LINE, x))
        )
        sends += 1
    for d in (2, 1, 3):
        pending.append(
            send(features, block(z, x), gather_send.at[sends], gather_recv.at[row], in_row(z, (x + d) % LINE))
        )
        sends += 1

    count = tile_count[0, 0]
    owners = [jnp.where(k < count, tile_rows[0, 0, k] // 2, -1) for k in range(SLOTS)]
    codes = [2 * k + tile_rows[0, 0, k] % 2 for k in range(SLOTS)]

    def code_of(dy, dh, dc):
        owner = in_col(dy, dh, dc)[1]
        code = 2 * SLOTS
        for k in range(SLOTS):
            code = jnp.where(owners[k] == owner, codes[k], code)
        return code

    code = {}
    for i, (dy, dc) in enumerate(RING):
        for dh in range(LINE):
            code[i, dh] = code_of(dy, dh, dc)
            flags_out[i, dh, :] = jnp.full((TILE,), code[i, dh] % 2, jnp.float32)
    for i, (dy, dc) in enumerate(OTHERS):
        pending.append(
            send(flags_out.at[i], flags_in.at[i], flags_send.at[i], flags_recv.at[i], in_col(dy, 0, dc))
        )

    near = [jnp.where(z % 2 == 0, z + 1, z - 1), jnp.where(z < 2, 2, 1), jnp.where(z < 2, 3, 0)]
    for z_from in near:
        held = block(z_from, x)
        slot = z_from * LINE + x
        pltpu.make_async_copy(held, held, gather_recv.at[slot]).wait()
        for d in (2, 1, 3):
            pending.append(
                send(held, held, gather_send.at[sends], gather_recv.at[slot], in_row(z, (x + d) % LINE))
            )
            sends += 1
    for z_from in [z] + near:
        for d in (1, 3, 2):
            x_from = (x + d) % LINE
            held = block(z_from, x_from)
            pltpu.make_async_copy(held, held, gather_recv.at[z_from * LINE + x_from]).wait()

    load_tiles.wait()
    load_mine.wait()
    products[SLOTS] = jnp.zeros((TILE, TILE), jnp.bfloat16)
    for k in range(SLOTS):
        inputs = gathered[tile_cols[0, 0, k]]
        products[k] = jnp.dot(tiles[k], inputs, preferred_element_type=jnp.float32).astype(jnp.bfloat16)

    for dh in FAR_FIRST:
        for i, (dy, dc) in enumerate(OTHERS):
            ring_out[dh, i] = products[code[i, dh] // 2]
            pending.append(
                send(ring_out.at[dh, i], ring_in.at[dh, i], ring_send.at[dh, i], ring_recv.at[dh, i], in_col(dy, 0, dc))
            )

    for i in range(len(OTHERS)):
        pltpu.make_async_copy(flags_in.at[i], flags_in.at[i], flags_recv.at[i]).wait()
    sums = None
    mine = len(OTHERS)
    for dh in FAR_FIRST:
        tile = products[code[mine, dh] // 2].astype(jnp.float32)
        second = flags_out[mine, dh, :][None, :] > 0.5
        sums = [jnp.where(second, 0.0, tile), jnp.where(second, tile, 0.0)]
        for i in range(len(OTHERS)):
            pltpu.make_async_copy(ring_in.at[dh, i], ring_in.at[dh, i], ring_recv.at[dh, i]).wait()
            tile = ring_in[dh, i].astype(jnp.float32)
            second = flags_in[i, dh, :][None, :] > 0.5
            sums = [sums[0] + jnp.where(second, 0.0, tile), sums[1] + jnp.where(second, tile, 0.0)]
        if dh:
            sums_out[dh - 1, 0] = sums[0].astype(jnp.bfloat16)
            sums_out[dh - 1, 1] = sums[1].astype(jnp.bfloat16)
            pending.append(
                send(
                    sums_out.at[dh - 1],
                    sums_in.at[dh - 1],
                    sums_send.at[dh - 1],
                    sums_recv.at[dh - 1],
                    in_col(0, dh, 0),
                )
            )

    for dh in (1, 3, 2):
        pltpu.make_async_copy(sums_in.at[dh - 1], sums_in.at[dh - 1], sums_recv.at[dh - 1]).wait()
        sums = [sums[s] + sums_in[dh - 1, s].astype(jnp.float32) for s in range(2)]
    low = jnp.concatenate(sums, axis=0).astype(jnp.bfloat16)
    mixed = jnp.maximum(jnp.dot(low, weight[...], preferred_element_type=jnp.float32), 0.0).astype(jnp.bfloat16)
    nodes = 2 * TILE
    place = (node_order[...] % nodes)[None, :]
    wanted = lax.broadcasted_iota(jnp.int32, (nodes, nodes), 0)
    moves = jnp.where(wanted == place, 1.0, 0.0).astype(jnp.bfloat16)
    out[...] = jnp.dot(moves, mixed, preferred_element_type=jnp.float32).astype(jnp.bfloat16)

    for copy in pending:
        copy.wait_send()


def on_device(features, weight, tile_values, tile_rows, tile_cols, tile_count, node_order):
    vmem = pl.BlockSpec(memory_space=pltpu.VMEM)
    smem = pl.BlockSpec(memory_space=pltpu.SMEM)
    hbm = pl.BlockSpec(memory_space=pl.ANY)
    dma = pltpu.SemaphoreType.DMA
    others = len(OTHERS)
    return pl.pallas_call(
        kernel,
        out_shape=jax.ShapeDtypeStruct(features.shape, features.dtype),
        in_specs=[hbm, vmem, hbm, smem, smem, smem, vmem],
        out_specs=vmem,
        scratch_shapes=[
            pltpu.VMEM((2 * LINE * LINE, TILE, TILE), jnp.bfloat16),
            pltpu.VMEM((SLOTS, TILE, TILE), jnp.bfloat16),
            pltpu.VMEM((SLOTS + 1, TILE, TILE), jnp.bfloat16),
            pltpu.VMEM((others + 1, 8, TILE), jnp.float32),
            pltpu.VMEM((others, 8, TILE), jnp.float32),
            pltpu.VMEM((LINE, others, TILE, TILE), jnp.bfloat16),
            pltpu.VMEM((LINE, others, TILE, TILE), jnp.bfloat16),
            pltpu.VMEM((LINE - 1, 2, TILE, TILE), jnp.bfloat16),
            pltpu.VMEM((LINE - 1, 2, TILE, TILE), jnp.bfloat16),
            dma((2,)),
            dma((15,)),
            dma((LINE * LINE,)),
            dma((others,)),
            dma((others,)),
            dma((LINE, others)),
            dma((LINE, others)),
            dma((LINE - 1,)),
            dma((LINE - 1,)),
        ],
        compiler_params=pltpu.CompilerParams(
            collective_id=0, has_side_effects=True, vmem_limit_bytes=32 * 2**20
        ),
        name="graph_convolution",
    )(features.reshape(2, TILE, TILE), weight, tile_values, tile_rows, tile_cols, tile_count, node_order)


def solution(mesh):
    return jax.shard_map(
        on_device,
        mesh=mesh,
        in_specs=(
            P(("col", "row"), None),
            P(),
            P("row", "col", None, None, None),
            P("row", "col", None),
            P("row", "col", None),
            P("row", "col"),
            P(("row", "col")),
        ),
        out_specs=P(("row", "col"), None),
        check_vma=False,
    )
```

```python
import jax
import jax.numpy as jnp
from jax import lax
from jax.experimental import pallas as pl
from jax.experimental.pallas import tpu as pltpu
from jax.sharding import PartitionSpec as P

MESH = pl.DeviceIdType.MESH
TILE = 128
HALF = TILE // 2
SLOTS = 16
LINE = 4
CELLS = LINE * LINE
RING = tuple((dy, dc) for dy in (2, 1, 3, 0) for dc in (1, 0))
OTHERS = RING[:-1]
MINE = len(OTHERS)
WAYS = ((1, 3), (3, 1))
PAIRS = tuple(((2, way), (back, 0)) for way, back in WAYS)
FAR, SUM, DIRECT = range(3)


def kernel(
    features_hbm,
    weight_hbm,
    tile_values_hbm,
    tile_rows_hbm,
    tile_cols_hbm,
    tile_count_hbm,
    node_order_hbm,
    out,
    features,
    weight,
    tiles,
    tile_rows,
    tile_cols,
    tile_count,
    node_order,
    gathered_a,
    gathered_b,
    products,
    moves,
    flags_out,
    flags_in,
    ring_out,
    ring_in,
    sums_out,
    sums_in,
    load_sem,
    gather_send,
    gather_recv,
    flags_send,
    flags_recv,
    ring_send,
    ring_recv,
    sums_send,
    sums_recv,
):
    row, col = lax.axis_index("row"), lax.axis_index("col")
    z, x = row // LINE, row % LINE
    y, h, core = col // 8, (col // 2) % LINE, col % 2
    first_lanes = lax.broadcasted_iota(jnp.int32, (TILE, TILE), 1) < HALF

    def in_row(z_at, x_at):
        return (z_at * LINE + x_at, col)

    def in_col(dy, dh, dc):
        return (row, ((y + dy) % LINE) * 8 + ((h + dh) % LINE) * 2 + (core + dc) % 2)

    gathered = (gathered_a, gathered_b)
    pending = []

    def send(src, dst, send_sem, recv_sem, device):
        copy = pltpu.make_async_remote_copy(
            src_ref=src, dst_ref=dst, send_sem=send_sem, recv_sem=recv_sem, device_id=device, device_id_type=MESH
        )
        copy.start()
        pending.append(copy)

    def arrived(ref, sem):
        pltpu.make_async_copy(ref, ref, sem).wait()

    def swap(value):
        return pltpu.roll(value, HALF, 1)

    barrier = pltpu.get_barrier_semaphore()
    partners = (
        [in_row((z + d) % LINE, x) for d in (1, 2, 3)]
        + [in_row(z, (x + d) % LINE) for d in (1, 2, 3)]
        + [in_col(dy, 0, dc) for dy, dc in OTHERS]
        + [in_col(0, dh, 0) for dh in (1, 3)]
    )
    for device in partners:
        pl.semaphore_signal(barrier, inc=1, device_id=device, device_id_type=MESH)

    loads = [
        pltpu.make_async_copy(src, dst, load_sem.at[i])
        for i, (src, dst) in enumerate(
            (
                (features_hbm, features),
                (tile_rows_hbm, tile_rows),
                (tile_cols_hbm, tile_cols),
                (tile_count_hbm, tile_count),
                (tile_values_hbm.at[0, 0], tiles),
                (node_order_hbm, node_order),
                (weight_hbm, weight),
            )
        )
    ]
    for load in loads:
        load.start()

    loads[0].wait()
    near_tile, next_tile = features[0].astype(jnp.float32), features[1].astype(jnp.float32)
    gathered_a[row] = jnp.where(first_lanes, near_tile, swap(next_tile)).astype(jnp.bfloat16)
    gathered_b[row] = jnp.where(first_lanes, swap(near_tile), next_tile).astype(jnp.bfloat16)
    pl.semaphore_wait(barrier, len(partners))

    sends = [0]

    def send_block(half, slot, device):
        block = gathered[half].at[slot]
        send(block, block, gather_send.at[sends[0]], gather_recv.at[half, slot], device)
        sends[0] += 1

    def send_along_z(half):
        for d in (1, 3, 2):
            send_block(half, row, in_row((z + d) % LINE, x))

    def send_along_x(half, z_from):
        for d in (2, 1, 3):
            send_block(half, z_from * LINE + x, in_row(z, (x + d) % LINE))

    near = [jnp.where(z % 2 == 0, z + 1, z - 1), jnp.where(z < 2, 2, 1), jnp.where(z < 2, 3, 0)]

    def forward(half):
        for z_from in near:
            slot = z_from * LINE + x
            arrived(gathered[half].at[slot], gather_recv.at[half, slot])
            send_along_x(half, z_from)

    def gather_end(half):
        for z_from in [z] + near:
            for d in (1, 3, 2):
                slot = z_from * LINE + (x + d) % LINE
                arrived(gathered[half].at[slot], gather_recv.at[half, slot])

    send_along_z(0)
    send_along_x(0, z)
    send_along_z(1)

    for load in loads[1:4]:
        load.wait()
    count = tile_count[0, 0]
    owners = [jnp.where(k < count, tile_rows[0, 0, k] // 2, -1) for k in range(SLOTS)]
    codes = [2 * k + tile_rows[0, 0, k] % 2 for k in range(SLOTS)]

    def code_of(dy, dh, dc):
        owner = in_col(dy, dh, dc)[1]
        code = 2 * SLOTS
        for k in range(SLOTS):
            code = jnp.where(owners[k] == owner, codes[k], code)
        return code

    forward(0)
    send_along_x(1, z)

    code = {(i, dh): code_of(dy, dh, dc) for i, (dy, dc) in enumerate(RING) for dh in range(LINE)}
    lanes = lax.broadcasted_iota(jnp.int32, (1, TILE), 1) < HALF
    for i in range(len(RING)):
        for half in range(2):
            for pair, (one, two) in enumerate(PAIRS[half]):
                second = jnp.where(lanes, code[i, one] % 2, code[i, two] % 2).astype(jnp.float32)
                flags_out[i, pl.ds(2 * half + pair, 1), :] = second
    for i, (dy, dc) in enumerate(OTHERS):
        send(flags_out.at[i], flags_in.at[i], flags_send.at[i], flags_recv.at[i], in_col(dy, 0, dc))

    forward(1)

    for load in loads[4:]:
        load.wait()

    def multiply(half):
        products[half, SLOTS] = jnp.zeros((TILE, TILE), jnp.bfloat16)
        for k in range(SLOTS):
            from_tile = tile_cols[0, 0, k]
            both = jnp.dot(tiles[k], gathered[half][from_tile // 2], preferred_element_type=jnp.float32)
            turned = swap(both)
            one = from_tile % 2 == 0
            wanted = jnp.where(first_lanes, jnp.where(one, both, turned), jnp.where(one, turned, both))
            products[half, k] = wanted.astype(jnp.bfloat16)

    def pair_of(half, pair, i):
        one, two = PAIRS[half][pair]
        return jnp.where(first_lanes, products[half, code[i, one] // 2], products[half, code[i, two] // 2])

    def send_ring(half):
        for pair in range(2):
            for i, (dy, dc) in enumerate(OTHERS):
                ring_out[half, pair, i] = pair_of(half, pair, i)
                send(
                    ring_out.at[half, pair, i],
                    ring_in.at[half, pair, i],
                    ring_send.at[half, pair, i],
                    ring_recv.at[half, pair, i],
                    in_col(dy, 0, dc),
                )

    gather_end(0)
    multiply(0)
    send_ring(0)
    gather_end(1)
    multiply(1)
    send_ring(1)

    nodes = 2 * TILE
    place = (node_order[...] % nodes)[None, :]
    wanted_rows = lax.broadcasted_iota(jnp.int32, (nodes, nodes), 0)
    moves[...] = jnp.where(wanted_rows == place, 1.0, 0.0).astype(jnp.bfloat16)

    for i in range(len(OTHERS)):
        arrived(flags_in.at[i], flags_recv.at[i])

    def sum_ring(half, pair):
        at = 2 * half + pair
        tile = pair_of(half, pair, MINE).astype(jnp.float32)
        second = flags_out[MINE, pl.ds(at, 1), :] > 0.5
        sums = [jnp.where(second, 0.0, tile), jnp.where(second, tile, 0.0)]
        for i in range(len(OTHERS)):
            arrived(ring_in.at[half, pair, i], ring_recv.at[half, pair, i])
            tile = ring_in[half, pair, i].astype(jnp.float32)
            second = flags_in[i, pl.ds(at, 1), :] > 0.5
            sums = [sums[0] + jnp.where(second, 0.0, tile), sums[1] + jnp.where(second, tile, 0.0)]
        return jnp.where(first_lanes, sums[0], swap(sums[1])), jnp.where(first_lanes, swap(sums[0]), sums[1])

    def send_sums(half, what, value):
        sums_out[half, what] = value.astype(jnp.bfloat16)
        way, back = WAYS[half]
        send(
            sums_out.at[half, what],
            sums_in.at[half, what],
            sums_send.at[half, what],
            sums_recv.at[half, what],
            in_col(0, back if what == DIRECT else way, 0),
        )

    def sums_from(half, what):
        arrived(sums_in.at[half, what], sums_recv.at[half, what])
        return sums_in[half, what].astype(jnp.float32)

    far, beside_a = sum_ring(0, 0)
    send_sums(0, FAR, far)
    direct, own_a = sum_ring(0, 1)
    send_sums(0, DIRECT, direct)
    far, beside_b = sum_ring(1, 0)
    send_sums(1, FAR, far)
    send_sums(0, SUM, beside_a + sums_from(0, FAR))
    direct, own_b = sum_ring(1, 1)
    send_sums(1, DIRECT, direct)
    send_sums(1, SUM, beside_b + sums_from(1, FAR))
    own_a = own_a + sums_from(0, DIRECT) + sums_from(0, SUM)
    own_b = own_b + sums_from(1, DIRECT) + sums_from(1, SUM)

    low = jnp.concatenate(
        [jnp.where(first_lanes, own_a, swap(own_b)), jnp.where(first_lanes, swap(own_a), own_b)], axis=0
    ).astype(jnp.bfloat16)
    mixed = jnp.maximum(jnp.dot(low, weight[...], preferred_element_type=jnp.float32), 0.0).astype(jnp.bfloat16)
    out[...] = jnp.dot(moves[...], mixed, preferred_element_type=jnp.float32).astype(jnp.bfloat16)

    for copy in pending:
        copy.wait_send()


def on_device(features, weight, tile_values, tile_rows, tile_cols, tile_count, node_order):
    dma = pltpu.SemaphoreType.DMA
    others = len(OTHERS)
    low = jnp.bfloat16
    return pl.pallas_call(
        kernel,
        out_shape=jax.ShapeDtypeStruct(features.shape, features.dtype),
        in_specs=[pl.BlockSpec(memory_space=pltpu.HBM)] * 7,
        out_specs=pl.BlockSpec(memory_space=pltpu.VMEM),
        scratch_shapes=[
            pltpu.VMEM((2, TILE, TILE), low),
            pltpu.VMEM(weight.shape, low),
            pltpu.VMEM((SLOTS, TILE, TILE), low),
            pltpu.SMEM(tile_rows.shape, jnp.int32),
            pltpu.SMEM(tile_cols.shape, jnp.int32),
            pltpu.SMEM(tile_count.shape, jnp.int32),
            pltpu.VMEM(node_order.shape, jnp.int32),
            pltpu.VMEM((CELLS, TILE, TILE), low),
            pltpu.VMEM((CELLS, TILE, TILE), low),
            pltpu.VMEM((2, SLOTS + 1, TILE, TILE), low),
            pltpu.VMEM((2 * TILE, 2 * TILE), low),
            pltpu.VMEM((others + 1, 8, TILE), jnp.float32),
            pltpu.VMEM((others, 8, TILE), jnp.float32),
            pltpu.VMEM((2, 2, others, TILE, TILE), low),
            pltpu.VMEM((2, 2, others, TILE, TILE), low),
            pltpu.VMEM((2, 3, TILE, TILE), low),
            pltpu.VMEM((2, 3, TILE, TILE), low),
            dma((7,)),
            dma((30,)),
            dma((2, CELLS)),
            dma((others,)),
            dma((others,)),
            dma((2, 2, others)),
            dma((2, 2, others)),
            dma((2, 3)),
            dma((2, 3)),
        ],
        compiler_params=pltpu.CompilerParams(
            collective_id=0, has_side_effects=True, vmem_limit_bytes=60 * 2**20
        ),
        name="graph_convolution",
    )(features.reshape(2, TILE, TILE), weight, tile_values, tile_rows, tile_cols, tile_count, node_order)


def solution(mesh):
    return jax.shard_map(
        on_device,
        mesh=mesh,
        in_specs=(
            P(("col", "row"), None),
            P(),
            P("row", "col", None, None, None),
            P("row", "col", None),
            P("row", "col", None),
            P("row", "col"),
            P(("row", "col")),
        ),
        out_specs=P(("row", "col"), None),
        check_vma=False,
    )
```

```python
import jax
import jax.numpy as jnp
from jax import lax
from jax.experimental import pallas as pl
from jax.experimental.pallas import tpu as pltpu
from jax.sharding import PartitionSpec as P

MESH = pl.DeviceIdType.MESH
TILE = 128
HALF = TILE // 2
SLOTS = 16
LINE = 4
CELLS = LINE * LINE
RING = tuple((dy, dc) for dy in (2, 1, 3, 0) for dc in (1, 0))
OTHERS = RING[:-1]
MINE = len(OTHERS)
PAIRS = ((2, 1), (3, 0))


def kernel(
    features_hbm,
    weight_hbm,
    tile_values_hbm,
    tile_rows_hbm,
    tile_cols_hbm,
    tile_count_hbm,
    node_order_hbm,
    out,
    features,
    weight,
    tiles,
    tile_rows,
    tile_cols,
    tile_count,
    node_order,
    gathered_a,
    gathered_b,
    products,
    moves,
    flags_out,
    flags_in,
    ring_out,
    ring_in,
    sums_out,
    sums_in,
    load_sem,
    gather_send,
    gather_recv,
    flags_send,
    flags_recv,
    ring_send,
    ring_recv,
    sums_send,
    sums_recv,
    far_sem,
):
    row, col = lax.axis_index("row"), lax.axis_index("col")
    z, x = row // LINE, row % LINE
    y, h, core = col // 8, (col // 2) % LINE, col % 2
    first_lanes = lax.broadcasted_iota(jnp.int32, (TILE, TILE), 1) < HALF

    def in_row(z_at, x_at):
        return (z_at * LINE + x_at, col)

    def in_col(dy, dh, dc):
        return (row, ((y + dy) % LINE) * 8 + ((h + dh) % LINE) * 2 + (core + dc) % 2)

    gathered = (gathered_a, gathered_b)
    pending = []

    def send(src, dst, send_sem, recv_sem, device):
        copy = pltpu.make_async_remote_copy(
            src_ref=src, dst_ref=dst, send_sem=send_sem, recv_sem=recv_sem, device_id=device, device_id_type=MESH
        )
        copy.start()
        pending.append(copy)

    def arrived(ref, sem):
        pltpu.make_async_copy(ref, ref, sem).wait()

    def swap(value):
        return pltpu.roll(value, HALF, 1)

    barrier = pltpu.get_barrier_semaphore()
    partners = (
        [in_row((z + d) % LINE, x) for d in (1, 2, 3)]
        + [in_row(z, (x + d) % LINE) for d in (1, 2, 3)]
        + [in_col(dy, 0, dc) for dy, dc in OTHERS]
        + [in_col(0, dh, 0) for dh in (1, 3)]
    )
    for device in partners:
        pl.semaphore_signal(barrier, inc=1, device_id=device, device_id_type=MESH)

    loads = [
        pltpu.make_async_copy(src, dst, load_sem.at[i])
        for i, (src, dst) in enumerate(
            (
                (features_hbm, features),
                (tile_rows_hbm, tile_rows),
                (tile_cols_hbm, tile_cols),
                (tile_count_hbm, tile_count),
                (tile_values_hbm.at[0, 0], tiles),
                (node_order_hbm, node_order),
                (weight_hbm, weight),
            )
        )
    ]
    for load in loads:
        load.start()

    loads[0].wait()
    near_tile, next_tile = features[0].astype(jnp.float32), features[1].astype(jnp.float32)
    gathered_a[row] = jnp.where(first_lanes, near_tile, swap(next_tile)).astype(jnp.bfloat16)
    gathered_b[row] = jnp.where(first_lanes, swap(near_tile), next_tile).astype(jnp.bfloat16)
    pl.semaphore_wait(barrier, len(partners))

    sends = [0]

    def send_block(half, slot, device):
        block = gathered[half].at[slot]
        send(block, block, gather_send.at[sends[0]], gather_recv.at[half, slot], device)
        sends[0] += 1

    def send_along_z(half):
        for d in (1, 3, 2):
            send_block(half, row, in_row((z + d) % LINE, x))

    def send_along_x(half, z_from):
        for d in (2, 1, 3):
            send_block(half, z_from * LINE + x, in_row(z, (x + d) % LINE))

    near = [jnp.where(z % 2 == 0, z + 1, z - 1), jnp.where(z < 2, 2, 1), jnp.where(z < 2, 3, 0)]

    def forward(half):
        for z_from in near:
            slot = z_from * LINE + x
            arrived(gathered[half].at[slot], gather_recv.at[half, slot])
            send_along_x(half, z_from)

    def gather_end(half):
        for z_from in [z] + near:
            for d in (1, 3, 2):
                slot = z_from * LINE + (x + d) % LINE
                arrived(gathered[half].at[slot], gather_recv.at[half, slot])

    send_along_z(0)
    send_along_x(0, z)
    send_along_z(1)
    pl.semaphore_signal(far_sem, inc=1, device_id=in_col(0, 3, 0), device_id_type=MESH)

    forward(0)
    send_along_x(1, z)
    forward(1)

    for load in loads[1:4]:
        load.wait()
    count = tile_count[0, 0]
    owners = [jnp.where(k < count, tile_rows[0, 0, k] // 2, -1) for k in range(SLOTS)]
    codes = [2 * k + tile_rows[0, 0, k] % 2 for k in range(SLOTS)]

    def code_of(dy, dh, dc):
        owner = in_col(dy, dh, dc)[1]
        code = 2 * SLOTS
        for k in range(SLOTS):
            code = jnp.where(owners[k] == owner, codes[k], code)
        return code

    code = {(i, dh): code_of(dy, dh, dc) for i, (dy, dc) in enumerate(RING) for dh in range(LINE)}
    lanes = lax.broadcasted_iota(jnp.int32, (1, TILE), 1) < HALF
    for i in range(len(RING)):
        for half in range(2):
            for pair, (one, two) in enumerate(PAIRS):
                second = jnp.where(lanes, code[i, one] % 2, code[i, two] % 2).astype(jnp.float32)
                flags_out[i, pl.ds(2 * half + pair, 1), :] = second
    for i, (dy, dc) in enumerate(OTHERS):
        send(flags_out.at[i], flags_in.at[i], flags_send.at[i], flags_recv.at[i], in_col(dy, 0, dc))

    for load in loads[4:]:
        load.wait()

    def multiply(half):
        products[half, SLOTS] = jnp.zeros((TILE, TILE), jnp.bfloat16)
        for k in range(SLOTS):
            from_tile = tile_cols[0, 0, k]
            both = jnp.dot(tiles[k], gathered[half][from_tile // 2], preferred_element_type=jnp.float32)
            turned = swap(both)
            one = from_tile % 2 == 0
            wanted = jnp.where(first_lanes, jnp.where(one, both, turned), jnp.where(one, turned, both))
            products[half, k] = wanted.astype(jnp.bfloat16)

    def pair_of(half, pair, i):
        one, two = PAIRS[pair]
        return jnp.where(first_lanes, products[half, code[i, one] // 2], products[half, code[i, two] // 2])

    def send_ring(half):
        for pair in range(2):
            for i, (dy, dc) in enumerate(OTHERS):
                ring_out[half, pair, i] = pair_of(half, pair, i)
                send(
                    ring_out.at[half, pair, i],
                    ring_in.at[half, pair, i],
                    ring_send.at[half, pair, i],
                    ring_recv.at[half, pair, i],
                    in_col(dy, 0, dc),
                )

    gather_end(0)
    multiply(0)
    send_ring(0)
    gather_end(1)
    multiply(1)
    send_ring(1)

    nodes = 2 * TILE
    place = (node_order[...] % nodes)[None, :]
    wanted_rows = lax.broadcasted_iota(jnp.int32, (nodes, nodes), 0)
    moves[...] = jnp.where(wanted_rows == place, 1.0, 0.0).astype(jnp.bfloat16)

    for i in range(len(OTHERS)):
        arrived(flags_in.at[i], flags_recv.at[i])

    def sum_ring(half, pair):
        at = 2 * half + pair
        tile = pair_of(half, pair, MINE).astype(jnp.float32)
        second = flags_out[MINE, pl.ds(at, 1), :] > 0.5
        sums = [jnp.where(second, 0.0, tile), jnp.where(second, tile, 0.0)]
        for i in range(len(OTHERS)):
            arrived(ring_in.at[half, pair, i], ring_recv.at[half, pair, i])
            tile = ring_in[half, pair, i].astype(jnp.float32)
            second = flags_in[i, pl.ds(at, 1), :] > 0.5
            sums = [sums[0] + jnp.where(second, 0.0, tile), sums[1] + jnp.where(second, tile, 0.0)]
        return jnp.where(first_lanes, sums[0], swap(sums[1])), jnp.where(first_lanes, swap(sums[0]), sums[1])

    def send_sums(half, dh, value):
        sums_out[half, dh - 1] = value.astype(jnp.bfloat16)
        send(
            sums_out.at[half, dh - 1],
            sums_in.at[half, dh - 1],
            sums_send.at[half, dh - 1],
            sums_recv.at[half, dh - 1],
            in_col(0, dh, 0),
        )

    pl.semaphore_wait(far_sem, 1)
    own = []
    for half in range(2):
        far, near_sum = sum_ring(half, 0)
        send_sums(half, 2, far)
        send_sums(half, 1, near_sum)
        near_sum, mine = sum_ring(half, 1)
        send_sums(half, 3, near_sum)
        own.append(mine)
    for half in range(2):
        for dh in (1, 3, 2):
            arrived(sums_in.at[half, dh - 1], sums_recv.at[half, dh - 1])
            own[half] = own[half] + sums_in[half, dh - 1].astype(jnp.float32)
    own_a, own_b = own

    low = jnp.concatenate(
        [jnp.where(first_lanes, own_a, swap(own_b)), jnp.where(first_lanes, swap(own_a), own_b)], axis=0
    ).astype(jnp.bfloat16)
    mixed = jnp.maximum(jnp.dot(low, weight[...], preferred_element_type=jnp.float32), 0.0).astype(jnp.bfloat16)
    out[...] = jnp.dot(moves[...], mixed, preferred_element_type=jnp.float32).astype(jnp.bfloat16)

    for copy in pending:
        copy.wait_send()


def on_device(features, weight, tile_values, tile_rows, tile_cols, tile_count, node_order):
    dma = pltpu.SemaphoreType.DMA
    others = len(OTHERS)
    low = jnp.bfloat16
    operands = (features.reshape(2, TILE, TILE), weight, tile_values, tile_rows, tile_cols, tile_count, node_order)
    return pl.pallas_call(
        kernel,
        out_shape=pltpu.VMEM(features.shape, features.dtype),
        in_specs=[pl.BlockSpec(memory_space=pltpu.HBM)] * 7,
        out_specs=pl.BlockSpec(memory_space=pltpu.VMEM),
        scratch_shapes=[
            pltpu.VMEM((2, TILE, TILE), low),
            pltpu.VMEM(weight.shape, low),
            pltpu.VMEM((SLOTS, TILE, TILE), low),
            pltpu.SMEM(tile_rows.shape, jnp.int32),
            pltpu.SMEM(tile_cols.shape, jnp.int32),
            pltpu.SMEM(tile_count.shape, jnp.int32),
            pltpu.VMEM(node_order.shape, jnp.int32),
            pltpu.VMEM((CELLS, TILE, TILE), low),
            pltpu.VMEM((CELLS, TILE, TILE), low),
            pltpu.VMEM((2, SLOTS + 1, TILE, TILE), low),
            pltpu.VMEM((2 * TILE, 2 * TILE), low),
            pltpu.VMEM((others + 1, 8, TILE), jnp.float32),
            pltpu.VMEM((others, 8, TILE), jnp.float32),
            pltpu.VMEM((2, 2, others, TILE, TILE), low),
            pltpu.VMEM((2, 2, others, TILE, TILE), low),
            pltpu.VMEM((2, 3, TILE, TILE), low),
            pltpu.VMEM((2, 3, TILE, TILE), low),
            dma((7,)),
            dma((30,)),
            dma((2, CELLS)),
            dma((others,)),
            dma((others,)),
            dma((2, 2, others)),
            dma((2, 2, others)),
            dma((2, 3)),
            dma((2, 3)),
            pltpu.SemaphoreType.REGULAR,
        ],
        compiler_params=pltpu.CompilerParams(
            collective_id=0, has_side_effects=True, vmem_limit_bytes=32 * 2**20
        ),
        name="graph_convolution",
    )(
        *(operand if operand is tile_count else pltpu.with_memory_space_constraint(operand, pltpu.HBM) for operand in operands)
    )


def solution(mesh):
    return jax.shard_map(
        on_device,
        mesh=mesh,
        in_specs=(
            P(("col", "row"), None),
            P(),
            P("row", "col", None, None, None),
            P("row", "col", None),
            P("row", "col", None),
            P("row", "col"),
            P(("row", "col")),
        ),
        out_specs=P(("row", "col"), None),
        check_vma=False,
    )
```

```python
import jax
import jax.numpy as jnp
from jax import lax
from jax.experimental import pallas as pl
from jax.experimental.pallas import tpu as pltpu
from jax.sharding import PartitionSpec as P

MESH = pl.DeviceIdType.MESH
TILE = 128
HALF = TILE // 2
CHUNKS = 4
WIDTH = TILE // CHUNKS
SLOTS = 16
LAST = 3
LINE = 4
CELLS = LINE * LINE
RING = tuple((dy, dc) for dy in (2, 1, 3, 0) for dc in (1, 0))
OTHERS = RING[:-1]
MINE = len(OTHERS)
GROUPS = (2, 1, 3, 0)


def kernel(
    features_hbm,
    weight_hbm,
    tile_values_hbm,
    tile_rows_hbm,
    tile_cols_hbm,
    tile_count_hbm,
    node_order_hbm,
    out,
    features,
    weight,
    tiles,
    tile_rows,
    tile_cols,
    tile_count,
    node_order,
    gathered_0,
    gathered_1,
    gathered_2,
    gathered_3,
    products,
    picks,
    moves,
    flags_out,
    flags_in,
    ring_out,
    ring_in,
    sums_out,
    sums_in,
    load_sem,
    gather_send,
    gather_recv,
    flags_send,
    flags_recv,
    ring_send,
    ring_recv,
    sums_send,
    sums_recv,
    far_sem,
):
    row, col = lax.axis_index("row"), lax.axis_index("col")
    z, x = row // LINE, row % LINE
    y, h, core = col // 8, (col // 2) % LINE, col % 2
    group = lax.broadcasted_iota(jnp.int32, (TILE, TILE), 1) // WIDTH
    half_group = lax.broadcasted_iota(jnp.int32, (HALF, TILE), 1) // WIDTH

    def in_row(z_at, x_at):
        return (z_at * LINE + x_at, col)

    def in_col(dy, dh, dc):
        return (row, ((y + dy) % LINE) * 8 + ((h + dh) % LINE) * 2 + (core + dc) % 2)

    gathered = (gathered_0, gathered_1, gathered_2, gathered_3)
    pending = []

    def send(src, dst, send_sem, recv_sem, device):
        copy = pltpu.make_async_remote_copy(
            src_ref=src, dst_ref=dst, send_sem=send_sem, recv_sem=recv_sem, device_id=device, device_id_type=MESH
        )
        copy.start()
        pending.append(copy)

    def arrived(ref, sem):
        pltpu.make_async_copy(ref, ref, sem).wait()

    def by_group(groups, pieces):
        value = pieces[0]
        for m in range(1, CHUNKS):
            value = jnp.where(groups == m, pieces[m], value)
        return value

    def shift(value, groups):
        return pltpu.roll(value, groups % CHUNKS * WIDTH, 1) if groups % CHUNKS else value

    barrier = pltpu.get_barrier_semaphore()
    partners = (
        [in_row((z + d) % LINE, x) for d in (1, 2, 3)]
        + [in_row(z, (x + d) % LINE) for d in (1, 2, 3)]
        + [in_col(dy, 0, dc) for dy, dc in OTHERS]
        + [in_col(0, dh, 0) for dh in (1, 3)]
    )
    for device in partners:
        pl.semaphore_signal(barrier, inc=1, device_id=device, device_id_type=MESH)

    loads = [
        pltpu.make_async_copy(src, dst, load_sem.at[i])
        for i, (src, dst) in enumerate(
            (
                (features_hbm, features),
                (tile_rows_hbm, tile_rows),
                (tile_cols_hbm, tile_cols),
                (tile_count_hbm, tile_count),
                (tile_values_hbm.at[0, 0], tiles),
                (node_order_hbm, node_order),
                (weight_hbm, weight),
            )
        )
    ]
    for load in loads:
        load.start()

    from_lane = lax.broadcasted_iota(jnp.int32, (TILE, 2 * TILE), 0)
    to_lane = lax.broadcasted_iota(jnp.int32, (TILE, 2 * TILE), 1)
    for s in range(2):
        wanted_lane = (2 * s + to_lane // TILE) * WIDTH + to_lane % WIDTH
        picks[s] = jnp.where(from_lane == wanted_lane, 1.0, 0.0).astype(jnp.bfloat16)

    loads[0].wait()
    quarters = [features[m // 2, pl.ds(m % 2 * HALF, HALF), :].astype(jnp.float32) for m in range(CHUNKS)]
    for c in range(CHUNKS):
        gathered[c][row] = by_group(half_group, [shift(quarters[m], m - c) for m in range(CHUNKS)]).astype(jnp.bfloat16)
    pl.semaphore_wait(barrier, len(partners))

    sends = [0]

    def send_block(c, slot, device):
        block = gathered[c].at[slot]
        send(block, block, gather_send.at[sends[0]], gather_recv.at[c, slot], device)
        sends[0] += 1

    def send_along_z(c, x_from):
        for d in (1, 3, 2):
            send_block(c, z * LINE + x_from, in_row((z + d) % LINE, x))

    def send_along_x(c, z_from):
        for d in (2, 1, 3):
            send_block(c, z_from * LINE + x, in_row(z, (x + d) % LINE))

    def block_arrived(c, slot):
        arrived(gathered[c].at[slot], gather_recv.at[c, slot])

    near = [jnp.where(z % 2 == 0, z + 1, z - 1), jnp.where(z < 2, 2, 1), jnp.where(z < 2, 3, 0)]

    def forward(c):
        for z_from in near:
            block_arrived(c, z_from * LINE + x)
            send_along_x(c, z_from)

    def forward_last():
        send_along_z(LAST, x)
        for d in (1, 3, 2):
            x_from = (x + d) % LINE
            block_arrived(LAST, z * LINE + x_from)
            send_along_z(LAST, x_from)

    def gather_end(c):
        for z_from in [z] + near if c != LAST else near:
            for d in (1, 3, 2) if c != LAST else (0, 1, 3, 2):
                block_arrived(c, z_from * LINE + (x + d) % LINE)

    send_along_z(0, x)
    send_along_x(0, z)
    send_along_x(LAST, z)
    send_along_z(1, x)
    send_along_z(2, x)
    pl.semaphore_signal(far_sem, inc=1, device_id=in_col(0, 3, 0), device_id_type=MESH)

    for load in loads[1:4]:
        load.wait()
    count = tile_count[0, 0]
    owners = [jnp.where(k < count, tile_rows[0, 0, k] // 2, -1) for k in range(SLOTS)]
    codes = [2 * k + tile_rows[0, 0, k] % 2 for k in range(SLOTS)]

    def code_of(dy, dh, dc):
        owner = in_col(dy, dh, dc)[1]
        code = 2 * SLOTS
        for k in range(SLOTS):
            code = jnp.where(owners[k] == owner, codes[k], code)
        return code

    code = {(i, dh): code_of(dy, dh, dc) for i, (dy, dc) in enumerate(RING) for dh in range(LINE)}
    row_group = lax.broadcasted_iota(jnp.int32, (1, TILE), 1) // WIDTH
    for i in range(len(RING)):
        second = by_group(row_group, [code[i, dh] % 2 for dh in GROUPS])
        flags_out[i, pl.ds(0, 1), :] = second.astype(jnp.float32)
    for i, (dy, dc) in enumerate(OTHERS):
        send(flags_out.at[i], flags_in.at[i], flags_send.at[i], flags_recv.at[i], in_col(dy, 0, dc))

    forward(0)
    send_along_x(1, z)
    forward_last()
    forward(1)
    send_along_x(2, z)
    forward(2)

    nodes = 2 * TILE
    for load in loads[4:]:
        load.wait()
    place = (node_order[...] % nodes)[None, :]
    wanted_rows = lax.broadcasted_iota(jnp.int32, (nodes, nodes), 0)
    moves[...] = jnp.where(wanted_rows == place, 1.0, 0.0).astype(jnp.bfloat16)

    def multiply(c):
        products[c, SLOTS] = jnp.zeros((TILE, TILE), jnp.bfloat16)
        for k in range(SLOTS):
            tile = tile_cols[0, 0, k]
            picked = jnp.dot(gathered[c][tile // 2], picks[tile % 2], preferred_element_type=jnp.float32)
            inputs = jnp.concatenate([picked[:, :TILE], picked[:, TILE:]], axis=0).astype(jnp.bfloat16)
            products[c, k] = jnp.dot(tiles[k], inputs, preferred_element_type=jnp.float32).astype(jnp.bfloat16)

    def tiles_for(c, i):
        return by_group(group, [products[c, code[i, dh] // 2] for dh in GROUPS])

    def send_ring(c):
        gather_end(c)
        multiply(c)
        for i, (dy, dc) in enumerate(OTHERS):
            ring_out[c, i] = tiles_for(c, i)
            send(ring_out.at[c, i], ring_in.at[c, i], ring_send.at[c, i], ring_recv.at[c, i], in_col(dy, 0, dc))

    def sum_ring(c):
        tile = tiles_for(c, MINE).astype(jnp.float32)
        second = flags_out[MINE, pl.ds(0, 1), :] > 0.5
        sums = [jnp.where(second, 0.0, tile), jnp.where(second, tile, 0.0)]
        for i in range(len(OTHERS)):
            arrived(ring_in.at[c, i], ring_recv.at[c, i])
            tile = ring_in[c, i].astype(jnp.float32)
            second = flags_in[i, pl.ds(0, 1), :] > 0.5
            sums = [sums[0] + jnp.where(second, 0.0, tile), sums[1] + jnp.where(second, tile, 0.0)]
        rows = [sums[m // 2][m % 2 * HALF : m % 2 * HALF + HALF] for m in range(CHUNKS)]
        return [by_group(half_group, [shift(rows[m], m - g) for m in range(CHUNKS)]) for g in range(LINE)]

    own = []

    def send_sums(c):
        sums = sum_ring(c)
        for g, dh in enumerate(GROUPS[:-1]):
            sums_out[c, g] = sums[g].astype(jnp.bfloat16)
            send(sums_out.at[c, g], sums_in.at[c, g], sums_send.at[c, g], sums_recv.at[c, g], in_col(0, dh, 0))
        own.append(sums[-1])

    send_ring(0)
    send_ring(1)
    send_ring(2)
    for i in range(len(OTHERS)):
        arrived(flags_in.at[i], flags_recv.at[i])
    pl.semaphore_wait(far_sem, 1)
    send_sums(0)
    send_ring(3)
    send_sums(1)
    send_sums(2)
    send_sums(3)
    for c in range(CHUNKS):
        for g in (1, 2, 0):
            arrived(sums_in.at[c, g], sums_recv.at[c, g])
            own[c] = own[c] + sums_in[c, g].astype(jnp.float32)

    low = jnp.concatenate(
        [by_group(half_group, [shift(own[c], c - m) for c in range(CHUNKS)]) for m in range(CHUNKS)], axis=0
    ).astype(jnp.bfloat16)
    mixed = jnp.maximum(jnp.dot(low, weight[...], preferred_element_type=jnp.float32), 0.0).astype(jnp.bfloat16)
    out[...] = jnp.dot(moves[...], mixed, preferred_element_type=jnp.float32).astype(jnp.bfloat16)

    for copy in pending:
        copy.wait_send()


def on_device(features, weight, tile_values, tile_rows, tile_cols, tile_count, node_order):
    dma = pltpu.SemaphoreType.DMA
    others = len(OTHERS)
    low = jnp.bfloat16
    operands = (features.reshape(2, TILE, TILE), weight, tile_values, tile_rows, tile_cols, tile_count, node_order)
    return pl.pallas_call(
        kernel,
        out_shape=pltpu.VMEM(features.shape, features.dtype),
        in_specs=[pl.BlockSpec(memory_space=pltpu.HBM)] * 7,
        out_specs=pl.BlockSpec(memory_space=pltpu.VMEM),
        scratch_shapes=[
            pltpu.VMEM((2, TILE, TILE), low),
            pltpu.VMEM(weight.shape, low),
            pltpu.VMEM((SLOTS, TILE, TILE), low),
            pltpu.SMEM(tile_rows.shape, jnp.int32),
            pltpu.SMEM(tile_cols.shape, jnp.int32),
            pltpu.SMEM(tile_count.shape, jnp.int32),
            pltpu.VMEM(node_order.shape, jnp.int32),
            *[pltpu.VMEM((CELLS, HALF, TILE), low)] * CHUNKS,
            pltpu.VMEM((CHUNKS, SLOTS + 1, TILE, TILE), low),
            pltpu.VMEM((2, TILE, 2 * TILE), low),
            pltpu.VMEM((2 * TILE, 2 * TILE), low),
            pltpu.VMEM((others + 1, 8, TILE), jnp.float32),
            pltpu.VMEM((others, 8, TILE), jnp.float32),
            pltpu.VMEM((CHUNKS, others, TILE, TILE), low),
            pltpu.VMEM((CHUNKS, others, TILE, TILE), low),
            pltpu.VMEM((CHUNKS, LINE - 1, HALF, TILE), low),
            pltpu.VMEM((CHUNKS, LINE - 1, HALF, TILE), low),
            dma((7,)),
            dma((60,)),
            dma((CHUNKS, CELLS)),
            dma((others,)),
            dma((others,)),
            dma((CHUNKS, others)),
            dma((CHUNKS, others)),
            dma((CHUNKS, LINE - 1)),
            dma((CHUNKS, LINE - 1)),
            pltpu.SemaphoreType.REGULAR,
        ],
        compiler_params=pltpu.CompilerParams(
            collective_id=0, has_side_effects=True, vmem_limit_bytes=32 * 2**20
        ),
        name="graph_convolution",
    )(
        *(operand if operand is tile_count else pltpu.with_memory_space_constraint(operand, pltpu.HBM) for operand in operands)
    )


def solution(mesh):
    return jax.shard_map(
        on_device,
        mesh=mesh,
        in_specs=(
            P(("col", "row"), None),
            P(),
            P("row", "col", None, None, None),
            P("row", "col", None),
            P("row", "col", None),
            P("row", "col"),
            P(("row", "col")),
        ),
        out_specs=P(("row", "col"), None),
        check_vma=False,
    )
```

```python
import jax
import jax.numpy as jnp
from jax import lax
from jax.experimental import pallas as pl
from jax.experimental.pallas import tpu as pltpu
from jax.sharding import PartitionSpec as P

MESH = pl.DeviceIdType.MESH
TILE = 128
HALF = TILE // 2
CHUNKS = 4
WIDTH = TILE // CHUNKS
FLAG_ROWS = 16
SLOTS = 16
LAST = 3
LINE = 4
CELLS = LINE * LINE
RING = tuple((dy, dc) for dy in (2, 1, 3, 0) for dc in (1, 0))
OTHERS = RING[:-1]
MINE = len(OTHERS)
GROUPS = (2, 1, 3, 0)


def kernel(
    features_hbm,
    weight_hbm,
    tile_values_hbm,
    tile_rows_hbm,
    tile_cols_hbm,
    tile_count_hbm,
    node_order_hbm,
    out,
    features,
    weight,
    tiles,
    tile_rows,
    tile_cols,
    tile_count,
    node_order,
    gathered_0,
    gathered_1,
    gathered_2,
    gathered_3,
    products,
    picks,
    moves,
    ring_out,
    ring_in,
    sums_out,
    sums_in,
    load_sem,
    gather_send,
    gather_recv,
    ring_send,
    ring_recv,
    sums_send,
    sums_recv,
    far_sem,
):
    row, col = lax.axis_index("row"), lax.axis_index("col")
    z, x = row // LINE, row % LINE
    y, h, core = col // 8, (col // 2) % LINE, col % 2
    group = lax.broadcasted_iota(jnp.int32, (TILE, TILE), 1) // WIDTH
    half_group = lax.broadcasted_iota(jnp.int32, (HALF, TILE), 1) // WIDTH

    def in_row(z_at, x_at):
        return (z_at * LINE + x_at, col)

    def in_col(dy, dh, dc):
        return (row, ((y + dy) % LINE) * 8 + ((h + dh) % LINE) * 2 + (core + dc) % 2)

    def slot_of(c, row_at):
        return row_at if c == LAST else row_at % LINE * LINE + row_at // LINE

    gathered = (gathered_0, gathered_1, gathered_2, gathered_3)
    def send(src, dst, send_sem, recv_sem, device):
        copy = pltpu.make_async_remote_copy(
            src_ref=src, dst_ref=dst, send_sem=send_sem, recv_sem=recv_sem, device_id=device, device_id_type=MESH
        )
        copy.start()

    def arrived(ref, sem):
        pltpu.make_async_copy(ref, ref, sem).wait()

    def by_group(groups, pieces):
        value = pieces[0]
        for m in range(1, CHUNKS):
            value = jnp.where(groups == m, pieces[m], value)
        return value

    def shift(value, groups):
        return pltpu.roll(value, groups % CHUNKS * WIDTH, 1) if groups % CHUNKS else value

    barrier = pltpu.get_barrier_semaphore()
    partners = (
        [in_row((z + d) % LINE, x) for d in (1, 2, 3)]
        + [in_row(z, (x + d) % LINE) for d in (1, 2, 3)]
        + [in_col(dy, 0, dc) for dy, dc in OTHERS]
        + [in_col(0, dh, 0) for dh in (1, 3)]
    )
    for device in partners:
        pl.semaphore_signal(barrier, inc=1, device_id=device, device_id_type=MESH)

    loads = [
        pltpu.make_async_copy(src, dst, load_sem.at[i])
        for i, (src, dst) in enumerate(
            (
                (features_hbm, features),
                (tile_rows_hbm, tile_rows),
                (tile_cols_hbm, tile_cols),
                (tile_count_hbm, tile_count),
                (tile_values_hbm.at[0, 0], tiles),
                (node_order_hbm, node_order),
                (weight_hbm, weight),
            )
        )
    ]
    for load in loads:
        load.start()

    from_lane = lax.broadcasted_iota(jnp.int32, (TILE, 2 * TILE), 0)
    to_lane = lax.broadcasted_iota(jnp.int32, (TILE, 2 * TILE), 1)
    for s in range(2):
        wanted_lane = (2 * s + to_lane // TILE) * WIDTH + to_lane % WIDTH
        picks[s] = jnp.where(from_lane == wanted_lane, 1.0, 0.0).astype(jnp.bfloat16)

    loads[0].wait()
    quarters = [features[m // 2, pl.ds(m % 2 * HALF, HALF), :].astype(jnp.float32) for m in range(CHUNKS)]
    for c in range(CHUNKS):
        gathered[c][slot_of(c, row)] = by_group(half_group, [shift(quarters[m], m - c) for m in range(CHUNKS)]).astype(jnp.bfloat16)
    pl.semaphore_wait(barrier, len(partners))

    def send_mine(c):
        mine = gathered[c].at[slot_of(c, row)]
        for d in (2, 1, 3) if c == LAST else (1, 3, 2):
            to = in_row(z, (x + d) % LINE) if c == LAST else in_row((z + d) % LINE, x)
            send(mine, mine, gather_send.at[c, 0], gather_recv.at[c, 0], to)

    def forward(c):
        arrived(gathered[c].at[pl.ds(0, LINE - 1)], gather_recv.at[c, 0])
        line = gathered[c].at[pl.ds(slot_of(c, row) // LINE * LINE, LINE)]
        for d in (1, 3, 2) if c == LAST else (2, 1, 3):
            to = in_row((z + d) % LINE, x) if c == LAST else in_row(z, (x + d) % LINE)
            send(line, line, gather_send.at[c, 1], gather_recv.at[c, 1], to)

    def mine_sent(c):
        arrived(gathered[c].at[pl.ds(0, LINE - 1)], gather_send.at[c, 0])

    def line_sent(c):
        arrived(gathered[c].at[pl.ds(0, CELLS - LINE)], gather_send.at[c, 1])

    def gather_end(c):
        arrived(gathered[c].at[pl.ds(0, CELLS - LINE)], gather_recv.at[c, 1])

    send_mine(0)
    send_mine(3)
    send_mine(1)
    send_mine(2)
    pl.semaphore_signal(far_sem, inc=1, device_id=in_col(0, 3, 0), device_id_type=MESH)

    for load in loads[1:4]:
        load.wait()
    count = tile_count[0, 0]
    owners = [jnp.where(k < count, tile_rows[0, 0, k] // 2, -1) for k in range(SLOTS)]
    codes = [2 * k + tile_rows[0, 0, k] % 2 for k in range(SLOTS)]

    def code_of(dy, dh, dc):
        owner = in_col(dy, dh, dc)[1]
        code = 2 * SLOTS
        for k in range(SLOTS):
            code = jnp.where(owners[k] == owner, codes[k], code)
        return code

    code = {(i, dh): code_of(dy, dh, dc) for i, (dy, dc) in enumerate(RING) for dh in range(LINE)}
    row_group = lax.broadcasted_iota(jnp.int32, (FLAG_ROWS, TILE), 1) // WIDTH

    def flags_for(i):
        return by_group(row_group, [code[i, dh] % 2 for dh in GROUPS]).astype(jnp.float32)

    for i in range(len(OTHERS)):
        ring_out[0, i, pl.ds(TILE, FLAG_ROWS), :] = flags_for(i).astype(jnp.bfloat16)


    def multiply(c):
        products[c, SLOTS] = jnp.zeros((TILE, TILE), jnp.bfloat16)
        for k in range(SLOTS):
            tile = tile_cols[0, 0, k]
            picked = jnp.dot(gathered[c][slot_of(c, tile // 2)], picks[tile % 2], preferred_element_type=jnp.float32)
            inputs = jnp.concatenate([picked[:, :TILE], picked[:, TILE:]], axis=0).astype(jnp.bfloat16)
            products[c, k] = jnp.dot(tiles[k], inputs, preferred_element_type=jnp.float32).astype(jnp.bfloat16)

    def tiles_for(c, i):
        return by_group(group, [products[c, code[i, dh] // 2] for dh in GROUPS])

    def ring_rows(c):
        return pl.ds(0, TILE + FLAG_ROWS if c == 0 else TILE)

    def send_ring(c):
        gather_end(c)
        multiply(c)
        rows = ring_rows(c)
        for i, (dy, dc) in enumerate(OTHERS):
            ring_out[c, i, pl.ds(0, TILE), :] = tiles_for(c, i)
            send(ring_out.at[c, i, rows], ring_in.at[c, i, rows], ring_send.at[c], ring_recv.at[c], in_col(dy, 0, dc))

    def ring_sent(c):
        arrived(ring_out.at[c, :, ring_rows(c)], ring_send.at[c])

    def sum_ring(c):
        tile = tiles_for(c, MINE).astype(jnp.float32)
        second = flags_for(MINE)[:1] > 0.5
        sums = [jnp.where(second, 0.0, tile), jnp.where(second, tile, 0.0)]
        arrived(ring_in.at[c, :, ring_rows(c)], ring_recv.at[c])
        for i in range(len(OTHERS)):
            tile = ring_in[c, i, pl.ds(0, TILE), :].astype(jnp.float32)
            second = ring_in[0, i, pl.ds(TILE, FLAG_ROWS), :].astype(jnp.float32)[:1] > 0.5
            sums = [sums[0] + jnp.where(second, 0.0, tile), sums[1] + jnp.where(second, tile, 0.0)]
        rows = [sums[m // 2][m % 2 * HALF : m % 2 * HALF + HALF] for m in range(CHUNKS)]
        return [by_group(half_group, [shift(rows[m], m - g) for m in range(CHUNKS)]) for g in range(LINE)]

    own = []

    def send_sums(c):
        sums = sum_ring(c)
        for g, dh in enumerate(GROUPS[:-1]):
            sums_out[c, g] = sums[g].astype(jnp.bfloat16)
            send(sums_out.at[c, g], sums_in.at[c, g], sums_send.at[c], sums_recv.at[c], in_col(0, dh, 0))
        own.append(sums[-1])

    forward(0)
    forward(3)
    forward(1)
    forward(2)
    loads[4].wait()
    send_ring(0)
    pl.semaphore_wait(far_sem, 1)
    send_ring(1)
    send_sums(0)
    send_ring(2)
    send_ring(3)
    send_sums(1)
    send_sums(2)
    nodes = 2 * TILE
    for load in loads[5:]:
        load.wait()
    place = (node_order[...] % nodes)[None, :]
    wanted_rows = lax.broadcasted_iota(jnp.int32, (nodes, nodes), 0)
    moves[...] = jnp.where(wanted_rows == place, 1.0, 0.0).astype(jnp.bfloat16)
    send_sums(3)
    mine_sent(0)
    mine_sent(1)
    mine_sent(2)
    mine_sent(3)
    line_sent(0)
    line_sent(1)
    line_sent(2)
    line_sent(3)
    ring_sent(0)
    ring_sent(1)
    ring_sent(2)
    ring_sent(3)
    for c in range(CHUNKS):
        arrived(sums_out.at[c], sums_send.at[c])
    for c in range(CHUNKS):
        arrived(sums_in.at[c], sums_recv.at[c])
        for g in range(LINE - 1):
            own[c] = own[c] + sums_in[c, g].astype(jnp.float32)

    low = jnp.concatenate(
        [by_group(half_group, [shift(own[c], c - m) for c in range(CHUNKS)]) for m in range(CHUNKS)], axis=0
    ).astype(jnp.bfloat16)
    mixed = jnp.maximum(jnp.dot(low, weight[...], preferred_element_type=jnp.float32), 0.0).astype(jnp.bfloat16)
    out[...] = jnp.dot(moves[...], mixed, preferred_element_type=jnp.float32).astype(jnp.bfloat16)


def on_device(features, weight, tile_values, tile_rows, tile_cols, tile_count, node_order):
    dma = pltpu.SemaphoreType.DMA
    others = len(OTHERS)
    low = jnp.bfloat16
    operands = (features.reshape(2, TILE, TILE), weight, tile_values, tile_rows, tile_cols, tile_count, node_order)
    return pl.pallas_call(
        kernel,
        out_shape=pltpu.VMEM(features.shape, features.dtype),
        in_specs=[pl.BlockSpec(memory_space=pltpu.HBM)] * 7,
        out_specs=pl.BlockSpec(memory_space=pltpu.VMEM),
        scratch_shapes=[
            pltpu.VMEM((2, TILE, TILE), low),
            pltpu.VMEM(weight.shape, low),
            pltpu.VMEM((SLOTS, TILE, TILE), low),
            pltpu.SMEM(tile_rows.shape, jnp.int32),
            pltpu.SMEM(tile_cols.shape, jnp.int32),
            pltpu.SMEM(tile_count.shape, jnp.int32),
            pltpu.VMEM(node_order.shape, jnp.int32),
            *[pltpu.VMEM((CELLS, HALF, TILE), low)] * CHUNKS,
            pltpu.VMEM((CHUNKS, SLOTS + 1, TILE, TILE), low),
            pltpu.VMEM((2, TILE, 2 * TILE), low),
            pltpu.VMEM((2 * TILE, 2 * TILE), low),
            pltpu.VMEM((CHUNKS, others, TILE + FLAG_ROWS, TILE), low),
            pltpu.VMEM((CHUNKS, others, TILE + FLAG_ROWS, TILE), low),
            pltpu.VMEM((CHUNKS, LINE - 1, HALF, TILE), low),
            pltpu.VMEM((CHUNKS, LINE - 1, HALF, TILE), low),
            dma((7,)),
            dma((CHUNKS, 2)),
            dma((CHUNKS, 2)),
            dma((CHUNKS,)),
            dma((CHUNKS,)),
            dma((CHUNKS,)),
            dma((CHUNKS,)),
            pltpu.SemaphoreType.REGULAR,
        ],
        compiler_params=pltpu.CompilerParams(
            collective_id=0, has_side_effects=True, vmem_limit_bytes=32 * 2**20
        ),
        name="graph_convolution",
    )(
        *(operand if operand is tile_count else pltpu.with_memory_space_constraint(operand, pltpu.HBM) for operand in operands)
    )


def solution(mesh):
    return jax.shard_map(
        on_device,
        mesh=mesh,
        in_specs=(
            P(("col", "row"), None),
            P(),
            P("row", "col", None, None, None),
            P("row", "col", None),
            P("row", "col", None),
            P("row", "col"),
            P(("row", "col")),
        ),
        out_specs=P(("row", "col"), None),
        check_vma=False,
    )
```

```python
import jax
import jax.numpy as jnp
from jax import lax
from jax.experimental import pallas as pl
from jax.experimental.pallas import tpu as pltpu
from jax.sharding import PartitionSpec as P

MESH = pl.DeviceIdType.MESH
TILE = 128
HALF = TILE // 2
CHUNKS = 4
WIDTH = TILE // CHUNKS
FLAG_ROWS = 16
SLOTS = 16
LAST = 3
LINE = 4
CELLS = LINE * LINE
RING = tuple((dy, dc) for dy in (2, 1, 3, 0) for dc in (1, 0))
OTHERS = RING[:-1]
MINE = len(OTHERS)
GROUPS = (2, 1, 3, 0)


def kernel(
    features_hbm,
    weight_hbm,
    tile_values_hbm,
    tile_rows_hbm,
    tile_cols_hbm,
    tile_count_hbm,
    node_order_hbm,
    out,
    features,
    weight,
    tiles,
    tile_rows,
    tile_cols,
    tile_count,
    node_order,
    gathered_0,
    gathered_1,
    gathered_2,
    gathered_3,
    products,
    picks,
    moves,
    ring_out,
    ring_in,
    sums_out,
    sums_in,
    load_sem,
    gather_send,
    gather_recv,
    ring_send,
    ring_recv,
    sums_send,
    sums_recv,
    far_sem,
):
    row, col = lax.axis_index("row"), lax.axis_index("col")
    z, x = row // LINE, row % LINE
    y, h, core = col // 8, (col // 2) % LINE, col % 2
    group = lax.broadcasted_iota(jnp.int32, (TILE, TILE), 1) // WIDTH
    half_group = lax.broadcasted_iota(jnp.int32, (HALF, TILE), 1) // WIDTH

    def in_row(z_at, x_at):
        return (z_at * LINE + x_at, col)

    def in_col(dy, dh, dc):
        return (row, ((y + dy) % LINE) * 8 + ((h + dh) % LINE) * 2 + (core + dc) % 2)

    def slot_of(c, row_at):
        return row_at if c == LAST else row_at % LINE * LINE + row_at // LINE

    gathered = (gathered_0, gathered_1, gathered_2, gathered_3)
    def send(src, dst, send_sem, recv_sem, device):
        copy = pltpu.make_async_remote_copy(
            src_ref=src, dst_ref=dst, send_sem=send_sem, recv_sem=recv_sem, device_id=device, device_id_type=MESH
        )
        copy.start()

    def arrived(ref, sem):
        pltpu.make_async_copy(ref, ref, sem).wait()

    def by_group(groups, pieces):
        value = pieces[0]
        for m in range(1, CHUNKS):
            value = jnp.where(groups == m, pieces[m], value)
        return value

    def shift(value, groups):
        return pltpu.roll(value, groups % CHUNKS * WIDTH, 1) if groups % CHUNKS else value

    barrier = pltpu.get_barrier_semaphore()
    partners = (
        [in_row((z + d) % LINE, x) for d in (1, 2, 3)]
        + [in_row(z, (x + d) % LINE) for d in (1, 2, 3)]
        + [in_col(dy, 0, dc) for dy, dc in OTHERS]
        + [in_col(0, dh, 0) for dh in (1, 3)]
    )
    for device in partners:
        pl.semaphore_signal(barrier, inc=1, device_id=device, device_id_type=MESH)

    loads = [
        pltpu.make_async_copy(src, dst, load_sem.at[i])
        for i, (src, dst) in enumerate(
            (
                (features_hbm, features),
                (tile_rows_hbm, tile_rows),
                (tile_cols_hbm, tile_cols),
                (tile_count_hbm, tile_count),
                (tile_values_hbm.at[0, 0], tiles),
                (node_order_hbm, node_order),
                (weight_hbm, weight),
            )
        )
    ]
    for load in loads:
        load.start()

    from_lane = lax.broadcasted_iota(jnp.int32, (TILE, 2 * TILE), 0)
    to_lane = lax.broadcasted_iota(jnp.int32, (TILE, 2 * TILE), 1)
    for s in range(2):
        wanted_lane = (2 * s + to_lane // TILE) * WIDTH + to_lane % WIDTH
        picks[s] = jnp.where(from_lane == wanted_lane, 1.0, 0.0).astype(jnp.bfloat16)

    loads[0].wait()
    quarters = [features[m // 2, pl.ds(m % 2 * HALF, HALF), :].astype(jnp.float32) for m in range(CHUNKS)]
    for c in range(CHUNKS):
        gathered[c][slot_of(c, row)] = by_group(half_group, [shift(quarters[m], m - c) for m in range(CHUNKS)]).astype(jnp.bfloat16)
    pl.semaphore_wait(barrier, len(partners))

    def send_mine(c):
        mine = gathered[c].at[slot_of(c, row)]
        for d in (2, 1, 3):
            to = in_row(z, (x + d) % LINE) if c == LAST else in_row((z + d) % LINE, x)
            send(mine, mine, gather_send.at[c, 0], gather_recv.at[c, 0], to)

    def forward(c):
        arrived(gathered[c].at[pl.ds(0, LINE - 1)], gather_recv.at[c, 0])
        line = gathered[c].at[pl.ds(slot_of(c, row) // LINE * LINE, LINE)]
        for d in (1, 3, 2) if c == LAST else (2, 1, 3):
            to = in_row((z + d) % LINE, x) if c == LAST else in_row(z, (x + d) % LINE)
            send(line, line, gather_send.at[c, 1], gather_recv.at[c, 1], to)

    def mine_sent(c):
        arrived(gathered[c].at[pl.ds(0, LINE - 1)], gather_send.at[c, 0])

    def line_sent(c):
        arrived(gathered[c].at[pl.ds(0, CELLS - LINE)], gather_send.at[c, 1])

    def gather_end(c):
        arrived(gathered[c].at[pl.ds(0, CELLS - LINE)], gather_recv.at[c, 1])

    send_mine(0)
    send_mine(3)
    send_mine(1)
    send_mine(2)
    pl.semaphore_signal(far_sem, inc=1, device_id=in_col(0, 3, 0), device_id_type=MESH)

    for load in loads[1:4]:
        load.wait()
    count = tile_count[0, 0]
    owners = [jnp.where(k < count, tile_rows[0, 0, k] // 2, -1) for k in range(SLOTS)]
    codes = [2 * k + tile_rows[0, 0, k] % 2 for k in range(SLOTS)]

    def code_of(dy, dh, dc):
        owner = in_col(dy, dh, dc)[1]
        code = 2 * SLOTS
        for k in range(SLOTS):
            code = jnp.where(owners[k] == owner, codes[k], code)
        return code

    code = {(i, dh): code_of(dy, dh, dc) for i, (dy, dc) in enumerate(RING) for dh in range(LINE)}
    row_group = lax.broadcasted_iota(jnp.int32, (FLAG_ROWS, TILE), 1) // WIDTH

    def flags_for(i):
        return by_group(row_group, [code[i, dh] % 2 for dh in GROUPS]).astype(jnp.float32)

    for i in range(len(OTHERS)):
        ring_out[0, i, pl.ds(TILE, FLAG_ROWS), :] = flags_for(i).astype(jnp.bfloat16)


    def multiply(c):
        products[c, SLOTS] = jnp.zeros((TILE, TILE), jnp.bfloat16)
        for k in range(SLOTS):
            tile = tile_cols[0, 0, k]
            picked = jnp.dot(gathered[c][slot_of(c, tile // 2)], picks[tile % 2], preferred_element_type=jnp.float32)
            inputs = jnp.concatenate([picked[:, :TILE], picked[:, TILE:]], axis=0).astype(jnp.bfloat16)
            products[c, k] = jnp.dot(tiles[k], inputs, preferred_element_type=jnp.float32).astype(jnp.bfloat16)

    def tiles_for(c, i):
        return by_group(group, [products[c, code[i, dh] // 2] for dh in GROUPS])

    def ring_rows(c):
        return pl.ds(0, TILE + FLAG_ROWS if c == 0 else TILE)

    def send_ring(c):
        gather_end(c)
        multiply(c)
        rows = ring_rows(c)
        for i, (dy, dc) in enumerate(OTHERS):
            ring_out[c, i, pl.ds(0, TILE), :] = tiles_for(c, i)
            send(ring_out.at[c, i, rows], ring_in.at[c, i, rows], ring_send.at[c], ring_recv.at[c], in_col(dy, 0, dc))

    def ring_sent(c):
        arrived(ring_out.at[c, :, ring_rows(c)], ring_send.at[c])

    def sum_ring(c):
        tile = tiles_for(c, MINE).astype(jnp.float32)
        second = flags_for(MINE)[:1] > 0.5
        sums = [jnp.where(second, 0.0, tile), jnp.where(second, tile, 0.0)]
        arrived(ring_in.at[c, :, ring_rows(c)], ring_recv.at[c])
        for i in range(len(OTHERS)):
            tile = ring_in[c, i, pl.ds(0, TILE), :].astype(jnp.float32)
            second = ring_in[0, i, pl.ds(TILE, FLAG_ROWS), :].astype(jnp.float32)[:1] > 0.5
            sums = [sums[0] + jnp.where(second, 0.0, tile), sums[1] + jnp.where(second, tile, 0.0)]
        rows = [sums[m // 2][m % 2 * HALF : m % 2 * HALF + HALF] for m in range(CHUNKS)]
        return [by_group(half_group, [shift(rows[m], m - g) for m in range(CHUNKS)]) for g in range(LINE)]

    own = []

    def send_sums(c):
        sums = sum_ring(c)
        for g, dh in enumerate(GROUPS[:-1]):
            sums_out[c, g] = sums[g].astype(jnp.bfloat16)
            send(sums_out.at[c, g], sums_in.at[c, g], sums_send.at[c], sums_recv.at[c], in_col(0, dh, 0))
        own.append(sums[-1])

    forward(0)
    forward(3)
    forward(1)
    forward(2)
    loads[4].wait()
    send_ring(0)
    pl.semaphore_wait(far_sem, 1)
    send_ring(1)
    send_sums(0)
    send_ring(2)
    send_ring(3)
    send_sums(1)
    send_sums(2)
    nodes = 2 * TILE
    for load in loads[5:]:
        load.wait()
    place = (node_order[...] % nodes)[None, :]
    wanted_rows = lax.broadcasted_iota(jnp.int32, (nodes, nodes), 0)
    moves[...] = jnp.where(wanted_rows == place, 1.0, 0.0).astype(jnp.bfloat16)
    send_sums(3)
    mine_sent(0)
    mine_sent(1)
    mine_sent(2)
    mine_sent(3)
    line_sent(0)
    line_sent(1)
    line_sent(2)
    line_sent(3)
    ring_sent(0)
    ring_sent(1)
    ring_sent(2)
    ring_sent(3)
    for c in range(CHUNKS):
        arrived(sums_out.at[c], sums_send.at[c])
    for c in range(CHUNKS):
        arrived(sums_in.at[c], sums_recv.at[c])
        for g in range(LINE - 1):
            own[c] = own[c] + sums_in[c, g].astype(jnp.float32)

    low = jnp.concatenate(
        [by_group(half_group, [shift(own[c], c - m) for c in range(CHUNKS)]) for m in range(CHUNKS)], axis=0
    ).astype(jnp.bfloat16)
    mixed = jnp.maximum(jnp.dot(low, weight[...], preferred_element_type=jnp.float32), 0.0).astype(jnp.bfloat16)
    out[...] = jnp.dot(moves[...], mixed, preferred_element_type=jnp.float32).astype(jnp.bfloat16)


def on_device(features, weight, tile_values, tile_rows, tile_cols, tile_count, node_order):
    dma = pltpu.SemaphoreType.DMA
    others = len(OTHERS)
    low = jnp.bfloat16
    operands = (features.reshape(2, TILE, TILE), weight, tile_values, tile_rows, tile_cols, tile_count, node_order)
    return pl.pallas_call(
        kernel,
        out_shape=pltpu.VMEM(features.shape, features.dtype),
        in_specs=[pl.BlockSpec(memory_space=pltpu.HBM)] * 7,
        out_specs=pl.BlockSpec(memory_space=pltpu.VMEM),
        scratch_shapes=[
            pltpu.VMEM((2, TILE, TILE), low),
            pltpu.VMEM(weight.shape, low),
            pltpu.VMEM((SLOTS, TILE, TILE), low),
            pltpu.SMEM(tile_rows.shape, jnp.int32),
            pltpu.SMEM(tile_cols.shape, jnp.int32),
            pltpu.SMEM(tile_count.shape, jnp.int32),
            pltpu.VMEM(node_order.shape, jnp.int32),
            *[pltpu.VMEM((CELLS, HALF, TILE), low)] * CHUNKS,
            pltpu.VMEM((CHUNKS, SLOTS + 1, TILE, TILE), low),
            pltpu.VMEM((2, TILE, 2 * TILE), low),
            pltpu.VMEM((2 * TILE, 2 * TILE), low),
            pltpu.VMEM((CHUNKS, others, TILE + FLAG_ROWS, TILE), low),
            pltpu.VMEM((CHUNKS, others, TILE + FLAG_ROWS, TILE), low),
            pltpu.VMEM((CHUNKS, LINE - 1, HALF, TILE), low),
            pltpu.VMEM((CHUNKS, LINE - 1, HALF, TILE), low),
            dma((7,)),
            dma((CHUNKS, 2)),
            dma((CHUNKS, 2)),
            dma((CHUNKS,)),
            dma((CHUNKS,)),
            dma((CHUNKS,)),
            dma((CHUNKS,)),
            pltpu.SemaphoreType.REGULAR,
        ],
        compiler_params=pltpu.CompilerParams(
            collective_id=0, has_side_effects=True, vmem_limit_bytes=32 * 2**20
        ),
        name="graph_convolution",
    )(
        *(operand if operand is tile_count else pltpu.with_memory_space_constraint(operand, pltpu.HBM) for operand in operands)
    )


def solution(mesh):
    return jax.shard_map(
        on_device,
        mesh=mesh,
        in_specs=(
            P(("col", "row"), None),
            P(),
            P("row", "col", None, None, None),
            P("row", "col", None),
            P("row", "col", None),
            P("row", "col"),
            P(("row", "col")),
        ),
        out_specs=P(("row", "col"), None),
        check_vma=False,
    )
```
